32 devices in a mesh: parts: 2 (over x), dp: 8 (over z, y), layer: 2 (over core).
Axes of the slice: x: 2, y: 2, z: 4, core: 2. Of those that a mesh axis runs over, the one named last changes fastest.
Arguments:
- train_acts: bfloat16 [16, 4, 256, 4096], P(('parts', 'dp'), 'layer'), parts along dimension 0, may hold values from -6 to 6
- train_grads: bfloat16 [16, 4, 256, 4096], P(('parts', 'dp'), 'layer'), parts along dimension 0
- train_lengths: int32 [16], P(('parts', 'dp')), parts along dimension 0, may hold values from 32 to 256, as said below
- query_log: bfloat16 [256, 4, 4096], P('dp', 'layer'), may hold values from -4 to 4
- proj_in: bfloat16 [4, 64, 4096], P('layer')
- proj_out: bfloat16 [4, 64, 4096], P('layer')
- basis_in: float32 [32, 64, 64], replicated, as said below
- basis_out: float32 [32, 64, 64], replicated, as said below
- layer_ids: int32 [4], P('layer'), may hold values from 0 to 31, as said below
Outputs:
- scores: float32 [16, 256], P(('parts', 'dp'), 'layer'), parts along dimension 0
The draws below stay inside these ranges and needn't reach their ends.
There are 2 independent parts, one for each index of `parts`. The reference program is written for one: setup_inputs(seed, part) draws one part's arguments, and reference() takes and returns one part's arrays. A program takes and returns all parts, laid end to end along the dimension named above; an argument that names none is the same for every part. Nothing has to cross between parts.
Inputs may be any that keep to these rules, and one draw needn't show every extreme that they name: `train_lengths`: at least one train sequence has exactly 256 live tokens and another exactly one eighth of 256. `layer_ids`: distinct layer numbers below 32; one of them is 31. `basis_in`: each [64, 64] matrix is orthogonal. `basis_out`: each [64, 64] matrix is orthogonal.
All inputs are finite; a program needn't handle non-finite values.
Results may differ from the reference program's by a relative error of at most 0.0041.
Values may be sent and summed in bfloat16 or wider, within the bound.
A program may use at most 128 MiB of HBM per device.

```python
import math
import jax
import jax.numpy as jnp
from jax import lax

D = 4096
NLAYERS = 32
R = 64
RR = 4096
LEN = 256
LAYERS = 4
TRAIN = 8
QUERY = 256


def reflect_frames(key, count, order):
    normals = jax.random.normal(key, (4, count, order), jnp.float32)
    normals = normals / jnp.sqrt(jnp.sum(normals * normals, axis=-1, keepdims=True))
    frames = jnp.broadcast_to(jnp.eye(order, dtype=jnp.float32), (count, order, order))
    for reflection in range(4):
        projected = jnp.sum(frames * normals[reflection][:, None, :], axis=-1)
        frames = frames - 2.0 * projected[:, :, None] * normals[reflection][:, None, :]
    return frames


def row_scaled(key, spread):
    key_rows, key_gain = jax.random.split(key)
    entries = jax.random.normal(key_rows, (LAYERS, R, D), jnp.float32) / math.sqrt(D)
    gains = jnp.exp(jax.random.uniform(key_gain, (LAYERS, R, 1), jnp.float32, -spread, spread))
    return entries * gains


def draw_proj_in(key, part):
    key = jax.random.fold_in(key, 3)
    return row_scaled(key, 1.1).astype(jnp.bfloat16)


def draw_proj_out(key, part):
    key = jax.random.fold_in(key, 4)
    return row_scaled(key, 1.1).astype(jnp.bfloat16)


def draw_train_grads(key, part):
    key = jax.random.fold_in(key, 5)
    key_base, key_jitter = jax.random.split(key, 2)
    ordinal = jnp.arange(TRAIN, dtype=jnp.float32) / max(TRAIN - 1, 1)
    base = jax.random.normal(key_base, (TRAIN, LAYERS, LEN, D), jnp.float32)
    ramp = 1.0 + 2.0 * ordinal
    jitter = jnp.exp(jax.random.uniform(key_jitter, (TRAIN, LAYERS, 1, 1), jnp.float32, -0.4, 0.4))
    return (base * ramp[:, None, None, None] * jitter).astype(jnp.bfloat16)


def draw_train_lengths(key, part):
    key = jax.random.fold_in(key, 7)
    key_one, key_two, key_three = jax.random.split(key, 3)
    minimum = LEN // 8
    counts = jax.random.randint(key_one, (TRAIN,), minimum, LEN + 1)
    longest = jax.random.randint(key_two, (), 0, TRAIN)
    stride_gap = jax.random.randint(key_three, (), 1, TRAIN)
    shortest = (longest + stride_gap) % TRAIN
    slot_index = jnp.arange(TRAIN, dtype=jnp.int32)
    counts = jnp.where(slot_index == longest, LEN, counts)
    counts = jnp.where(slot_index == shortest, minimum, counts)
    return counts.astype(jnp.int32)


def draw_layer_ids(key, part):
    key = jax.random.fold_in(key, 11)
    key_one, key_two = jax.random.split(key)
    remaining = jax.random.permutation(key_one, NLAYERS - 1)[:LAYERS - 1]
    position = jax.random.randint(key_two, (), 0, LAYERS)
    slot_index = jnp.arange(LAYERS, dtype=jnp.int32)
    shifted = jnp.where(slot_index < position, slot_index, slot_index - 1)
    chosen = remaining[jnp.clip(shifted, 0, LAYERS - 2)]
    return jnp.where(slot_index == position, NLAYERS - 1, chosen).astype(jnp.int32)


def draw_basis_in(key, part):
    key = jax.random.fold_in(key, 13)
    return reflect_frames(key, NLAYERS, R)


def draw_basis_out(key, part):
    key = jax.random.fold_in(key, 17)
    return reflect_frames(key, NLAYERS, R)


def block_scale(key, extent, cuts, low, high):
    level = 1.0
    for dim, parts in cuts:
        draws = jax.random.uniform(jax.random.fold_in(jax.random.fold_in(key, 6), dim), (parts,), jnp.float32, low / len(cuts), high / len(cuts))
        level = level * jnp.repeat(jnp.exp(draws), extent[dim] // parts).reshape((-1,) + (1,) * (len(extent) - 1 - dim))
    return level


def normal_values(own_key, dims, width, most, cuts=(), kind=jnp.bfloat16):
    values = jax.random.normal(own_key, dims, jnp.float32) * width
    if len(cuts) > 0:
        values = block_scale(own_key, dims, cuts, -0.22, 0.18) * values
    return jnp.clip(values, min=-most, max=most).astype(kind)


def setup_inputs(seed: int = 0, part: int = 0) -> dict:
    arg_keys = jax.random.split(jax.random.key(seed), 10)
    own_keys = jax.random.split(jax.random.fold_in(arg_keys[9], part), 10)
    train_acts = normal_values(own_keys[0], (TRAIN, LAYERS, LEN, D), 1.0, 6.0, ((0, 8), (1, 2)))
    train_grads = draw_train_grads(jax.random.fold_in(jax.random.fold_in(arg_keys[9], part), 71), part)
    train_lengths = draw_train_lengths(jax.random.fold_in(jax.random.fold_in(arg_keys[9], part), 71), part)
    query_log = normal_values(arg_keys[3], (QUERY, LAYERS, RR), 0.3, 4.0, ((0, 8), (1, 2)))
    proj_in = draw_proj_in(jax.random.fold_in(arg_keys[9], 71), part)
    proj_out = draw_proj_out(jax.random.fold_in(arg_keys[9], 71), part)
    basis_in = draw_basis_in(jax.random.fold_in(arg_keys[9], 71), part)
    basis_out = draw_basis_out(jax.random.fold_in(arg_keys[9], 71), part)
    layer_ids = draw_layer_ids(jax.random.fold_in(arg_keys[9], 71), part)
    return dict(train_acts=train_acts, train_grads=train_grads, train_lengths=train_lengths, query_log=query_log, proj_in=proj_in, proj_out=proj_out, basis_in=basis_in, basis_out=basis_out, layer_ids=layer_ids)


def rotate(frame_out, frame_in, matrices):
    highest = lax.Precision.HIGHEST
    left_turn = jnp.einsum('ca,scd->sad', frame_out, matrices, precision=highest)
    return jnp.einsum('sad,db->sab', left_turn, frame_in, precision=highest)


def reference(train_acts, train_grads, train_lengths, query_log, proj_in, proj_out, basis_in, basis_out, layer_ids):
    highest = lax.Precision.HIGHEST
    token_mask = (jnp.arange(LEN, dtype=jnp.int32)[None, :] < train_lengths[:, None]).astype(jnp.float32)
    selector = (layer_ids[:, None] == jnp.arange(NLAYERS, dtype=jnp.int32)[None, :]).astype(jnp.float32)
    frames_in = jnp.einsum('ln,nab->lab', selector, basis_in, precision=highest)
    frames_out = jnp.einsum('ln,nab->lab', selector, basis_out, precision=highest)
    scores = jnp.zeros((TRAIN, QUERY), jnp.float32)
    for level in range(LAYERS):
        activations = train_acts[:, level].astype(jnp.float32)
        gradients = train_grads[:, level].astype(jnp.float32)
        low_in = jnp.einsum('rd,std->srt', proj_in[level].astype(jnp.float32), activations)
        low_out = jnp.einsum('rd,std->srt', proj_out[level].astype(jnp.float32), gradients)
        low_out = low_out * token_mask[:, None, :]
        outer = jnp.einsum('sat,sbt->sab', low_out, low_in, precision=highest)
        turned = rotate(frames_out[level], frames_in[level], outer)
        energy = jnp.mean(turned * turned, axis=0)
        damping = 0.1 * jnp.mean(energy) + 1e-6
        train_rot = turned.astype(jnp.bfloat16).reshape(TRAIN, R * R)
        query_mat = query_log[:, level].astype(jnp.float32).reshape(QUERY, R, R)
        query_turn = rotate(frames_out[level], frames_in[level], query_mat)
        query_damped = (query_turn / (energy + damping)).astype(jnp.bfloat16).reshape(QUERY, R * R)
        scores = scores + jnp.dot(train_rot, query_damped.T, preferred_element_type=jnp.float32)
    return scores
```

```python
import functools

import jax
import jax.numpy as jnp
from jax import lax
from jax.experimental import pallas as pl
from jax.experimental.pallas import tpu as pltpu
from jax.sharding import PartitionSpec as P

F32 = jnp.float32
BF16 = jnp.bfloat16
MESH = pl.DeviceIdType.MESH
NN = (((1,), (0,)), ((), ()))
NT = (((1,), (1,)), ((), ()))


def dot(a, b, dims=NN):
    return lax.dot_general(a, b, dims, preferred_element_type=F32)


def split(a):
    hi = a.astype(BF16)
    return hi, (a - hi.astype(F32)).astype(BF16)


def dot3(a, b, dims=NN):
    ah, al = split(a)
    bh, bl = split(b)
    return dot(ah, bh, dims) + (dot(ah, bl, dims) + dot(al, bh, dims))


def kernel(
    n, layers, lens, lids, acts, grads, query, pin, pout, bin_, bout, out,
    abuf, gbuf, pibuf, pobuf, qbuf, bibuf, bobuf, tbuf, wbuf, sbuf, rbuf,
    load_sem, send_sem, recv_sem, send2_sem, recv2_sem,
):
    part = lax.axis_index("parts")
    me = lax.axis_index("dp")
    core = lax.axis_index("layer")
    half = n // layers
    mine = me // half
    rank = pibuf.shape[1]
    qpd = qbuf.shape[1]
    tokens = abuf.shape[1]

    barrier = pltpu.get_barrier_semaphore()
    for off in range(n):
        for lay in range(layers):
            if off == 0 and lay == 0:
                continue
            pl.semaphore_signal(
                barrier, inc=1,
                device_id=(part, lax.rem(me + off, n), lax.rem(core + lay, layers)),
                device_id_type=MESH,
            )

    loads = []

    def load(src, dst):
        c = pltpu.make_async_copy(src, dst, load_sem.at[len(loads)])
        c.start()
        loads.append(c)
        return c

    lp = []
    for l in range(2):
        a = load(pout.at[l], pobuf.at[l])
        b = load(grads.at[0, l], gbuf.at[l])
        c = load(pin.at[l], pibuf.at[l])
        d = load(acts.at[0, l], abuf.at[l])
        if l == 0:
            e = (load(bin_, bibuf), load(bout, bobuf))
        lp.append((a, b, c, d))
    lq = load(query, qbuf)

    length = lens[0]
    live = lax.broadcasted_iota(jnp.int32, (rank, tokens), 1) < length
    frames_in, frames_out, turned = [], [], []
    for l in range(2):
        a, b, c, d = lp[l]
        a.wait()
        b.wait()
        low_out = dot(pobuf[l], gbuf[l], NT)
        low_out = jnp.where(live, low_out, 0.0)
        c.wait()
        d.wait()
        low_in = dot(abuf[l], pibuf[l], NT)
        if l == 0:
            e[0].wait()
            e[1].wait()
        v = bibuf[lids[l]]
        u = bobuf[lids[l]]
        frames_in.append(v)
        frames_out.append(u)
        outer = dot3(low_out, low_in)
        turned.append(dot3(dot3(u.T, outer), v))
    tbuf[me] = jnp.concatenate(turned, axis=1).astype(BF16)

    peers = (n * layers) - 1
    pl.semaphore_wait(barrier, peers)

    def gather(off):
        to = lax.rem(me + off, n)
        return pltpu.make_async_remote_copy(
            src_ref=tbuf.at[me], dst_ref=tbuf.at[me],
            send_sem=send_sem.at[off - 1], recv_sem=recv_sem.at[off - 1],
            device_id=(part, to, core), device_id_type=MESH,
        )

    def arrived(off):
        frm = lax.rem(me + n - off, n)
        return pltpu.make_async_remote_copy(
            src_ref=tbuf.at[frm], dst_ref=tbuf.at[frm],
            send_sem=send_sem.at[off - 1], recv_sem=recv_sem.at[off - 1],
            device_id=(part, frm, core), device_id_type=MESH,
        )

    for off in range(1, n):
        gather(off).start()

    zero = jnp.zeros((rank, rank), F32)
    v0 = jnp.concatenate([frames_in[0], zero], axis=1)
    v1 = jnp.concatenate([zero, frames_in[1]], axis=1)
    right = jnp.concatenate([v0, v0, v1, v1], axis=0)
    lq.wait()

    for off in range(1, n):
        arrived(off).wait_recv()

    t = tbuf[...].astype(F32)
    energy = jnp.sum(t * t, axis=0) * (1.0 / n)
    first = lax.broadcasted_iota(jnp.int32, energy.shape, 1) < rank
    sum0 = jnp.sum(jnp.where(first, energy, 0.0))
    sum1 = jnp.sum(jnp.where(first, 0.0, energy))
    damping = jnp.where(first, sum0, sum1) * (0.1 / (rank * rank)) + 1e-6
    scaled = t * (1.0 / (energy + damping))[None]
    y = dot3(scaled.reshape(n * rank, 2 * rank), right, NT)
    wide = 2 * rank
    lanes = lax.broadcasted_iota(jnp.int32, (n, wide), 1) < rank
    total = None
    for l in range(2):
        yl = jnp.concatenate(
            [y[s * rank:(s + 1) * rank, l * wide:(l + 1) * wide] for s in range(n)], axis=1
        )
        w = dot3(frames_out[l], yl)
        for s in range(n):
            wbuf[l, s * rank:(s + 1) * rank, :] = w[:, s * wide:(s + 1) * wide]
        tiles = []
        for j in range(rank // 2):
            even = wbuf[l, pl.ds(2 * j, n, stride=rank), :]
            odd = wbuf[l, pl.ds(2 * j + 1, n, stride=rank), :]
            tiles.append(jnp.where(lanes, even, odd))
        flat = jnp.concatenate(tiles, axis=1)
        hi = flat.astype(BF16).astype(F32)
        both = jnp.concatenate([hi, flat - hi], axis=0).astype(BF16)
        p = dot(both, qbuf[l], NT)
        p = p[:n] + p[n:]
        total = p if total is None else total + p
    if qpd < 128:
        total = jnp.concatenate([total, jnp.zeros((n, 128 - qpd), F32)], axis=1)
    for s in range(n):
        sbuf[s] = total[s:s + 1]

    slot = core * half + lax.rem(me, half)

    def deliver(off):
        to = lax.rem(me + off, n)
        return pltpu.make_async_remote_copy(
            src_ref=sbuf.at[to], dst_ref=rbuf.at[slot],
            send_sem=send2_sem.at[off], recv_sem=recv2_sem.at[slot],
            device_id=(part, to, mine), device_id_type=MESH,
        )

    for off in range(1, n):
        deliver(off).start()

    @pl.when(mine == core)
    def _():
        rbuf[slot] = sbuf[me]

    @pl.when(mine != core)
    def _():
        deliver(0).start()

    for lay in range(layers):
        for j in range(half):
            src = core * half + j
            own = jnp.logical_and(src == me, core == lay)

            @pl.when(jnp.logical_not(own))
            def _(lay=lay, j=j):
                k = lay * half + j
                pltpu.make_async_remote_copy(
                    src_ref=sbuf.at[0], dst_ref=rbuf.at[k],
                    send_sem=send2_sem.at[0], recv_sem=recv2_sem.at[k],
                    device_id=(part, me, mine), device_id_type=MESH,
                ).wait_recv()

    pieces = []
    for j in range(half):
        acc = rbuf[j]
        for lay in range(1, layers):
            acc = acc + rbuf[lay * half + j]
        pieces.append(acc[:, :qpd])
    out[...] = jnp.concatenate(pieces, axis=1)

    for off in range(1, n):
        gather(off).wait_send()
        deliver(off).wait_send()

    @pl.when(mine != core)
    def _():
        deliver(0).wait_send()


def per_device(acts, grads, lens, query, pin, pout, bin_, bout, lids):
    n = lax.axis_size("dp")
    layers = lax.axis_size("layer")
    _, held, tokens, width = acts.shape
    rank = pin.shape[1]
    qpd = query.shape[0]
    query = jnp.swapaxes(query, 0, 1)
    hbm = pl.BlockSpec(memory_space=pl.ANY)
    smem = pl.BlockSpec(memory_space=pltpu.SMEM)
    return pl.pallas_call(
        functools.partial(kernel, n, layers),
        out_shape=jax.ShapeDtypeStruct((1, n * qpd // layers), F32),
        in_specs=[smem, smem] + [hbm] * 7,
        out_specs=pl.BlockSpec(memory_space=pltpu.VMEM),
        scratch_shapes=[
            pltpu.VMEM((held, tokens, width), BF16),
            pltpu.VMEM((held, tokens, width), BF16),
            pltpu.VMEM(pin.shape, BF16),
            pltpu.VMEM(pin.shape, BF16),
            pltpu.VMEM(query.shape, BF16),
            pltpu.VMEM(bin_.shape, F32),
            pltpu.VMEM(bout.shape, F32),
            pltpu.VMEM((n, rank, held * rank), BF16),
            pltpu.VMEM((held, n * rank, 2 * rank), F32),
            pltpu.VMEM((n, 1, 128), F32),
            pltpu.VMEM((n, 1, 128), F32),
            pltpu.SemaphoreType.DMA((11,)),
            pltpu.SemaphoreType.DMA((n - 1,)),
            pltpu.SemaphoreType.DMA((n - 1,)),
            pltpu.SemaphoreType.DMA((n,)),
            pltpu.SemaphoreType.DMA((n,)),
        ],
        compiler_params=pltpu.CompilerParams(
            collective_id=0, has_side_effects=True, vmem_limit_bytes=48 * 2**20
        ),
    )(lens, lids, acts, grads, query, pin, pout, bin_, bout)


def solution(mesh):
    return jax.shard_map(
        per_device,
        mesh=mesh,
        in_specs=(
            P(("parts", "dp"), "layer", None, None),
            P(("parts", "dp"), "layer", None, None),
            P(("parts", "dp")),
            P("dp", "layer", None),
            P("layer", None, None),
            P("layer", None, None),
            P(),
            P(),
            P("layer"),
        ),
        out_specs=P(("parts", "dp"), "layer"),
        check_vma=False,
    )
```

```python
import functools

import jax
import jax.numpy as jnp
from jax import lax
from jax.experimental import pallas as pl
from jax.experimental.pallas import tpu as pltpu
from jax.sharding import PartitionSpec as P

F32 = jnp.float32
BF16 = jnp.bfloat16
MESH = pl.DeviceIdType.MESH
NN = (((1,), (0,)), ((), ()))
NT = (((1,), (1,)), ((), ()))


def dot(a, b, dims=NN):
    return lax.dot_general(a, b, dims, preferred_element_type=F32)


def split(a):
    hi = a.astype(BF16)
    return hi, (a - hi.astype(F32)).astype(BF16)


def dot3(a, b, dims=NN):
    ah, al = split(a)
    bh, bl = split(b)
    return dot(ah, bh, dims) + (dot(ah, bl, dims) + dot(al, bh, dims))


def kernel(
    n, layers, lens, lids, acts, grads, query, pin, pout, bin_, bout, out,
    abuf, gbuf, pibuf, pobuf, xbuf, fbuf, qbuf, bibuf, bobuf, tbuf, wbuf, sbuf, rbuf,
    load_sem, send_sem, recv_sem, send2_sem, recv2_sem,
):
    part = lax.axis_index("parts")
    me = lax.axis_index("dp")
    core = lax.axis_index("layer")
    half = n // layers
    mine = me // half
    rank = pibuf.shape[1]
    qpd = query.shape[0]
    tokens = abuf.shape[1]

    barrier = pltpu.get_barrier_semaphore()
    for off in range(n):
        for lay in range(layers):
            if off == 0 and lay == 0:
                continue
            pl.semaphore_signal(
                barrier, inc=1,
                device_id=(part, lax.rem(me + off, n), lax.rem(core + lay, layers)),
                device_id_type=MESH,
            )

    loads = []

    def load(src, dst):
        c = pltpu.make_async_copy(src, dst, load_sem.at[len(loads)])
        c.start()
        loads.append(c)
        return c

    lp = []
    for l in range(2):
        a = load(pout.at[l], pobuf.at[l])
        b = load(grads.at[0, l], gbuf.at[l])
        c = load(pin.at[l], pibuf.at[l])
        d = load(acts.at[0, l], abuf.at[l])
        if l == 0:
            e = (load(bin_, bibuf), load(bout, bobuf))
        lp.append((a, b, c, d))
    lq = load(query, xbuf)

    length = lens[0]
    live = lax.broadcasted_iota(jnp.int32, (rank, tokens), 1) < length
    frames_in, frames_out, turned = [], [], []
    for l in range(2):
        a, b, c, d = lp[l]
        a.wait()
        b.wait()
        low_out = dot(pobuf[l], gbuf[l], NT)
        low_out = jnp.where(live, low_out, 0.0)
        c.wait()
        d.wait()
        low_in = dot(abuf[l], pibuf[l], NT)
        if l == 0:
            e[0].wait()
            e[1].wait()
        v = bibuf[lids[l]]
        u = bobuf[lids[l]]
        frames_in.append(v)
        frames_out.append(u)
        outer = dot3(low_out, low_in)
        turned.append(dot3(dot3(u.T, outer), v))
    tbuf[me] = jnp.concatenate(turned, axis=1).astype(BF16)

    peers = (n * layers) - 1
    pl.semaphore_wait(barrier, peers)

    def gather(off):
        to = lax.rem(me + off, n)
        return pltpu.make_async_remote_copy(
            src_ref=tbuf.at[me], dst_ref=tbuf.at[me],
            send_sem=send_sem.at[off - 1], recv_sem=recv_sem.at[off - 1],
            device_id=(part, to, core), device_id_type=MESH,
        )

    def arrived(off):
        frm = lax.rem(me + n - off, n)
        return pltpu.make_async_remote_copy(
            src_ref=tbuf.at[frm], dst_ref=tbuf.at[frm],
            send_sem=send_sem.at[off - 1], recv_sem=recv_sem.at[off - 1],
            device_id=(part, frm, core), device_id_type=MESH,
        )

    for off in range(1, n):
        gather(off).start()

    zero = jnp.zeros((rank, rank), F32)
    v0 = jnp.concatenate([frames_in[0], zero], axis=1)
    v1 = jnp.concatenate([zero, frames_in[1]], axis=1)
    right = jnp.concatenate([v0, v0, v1, v1], axis=0)
    lq.wait()
    rows = xbuf[...].reshape(2 * qpd, xbuf.shape[2])
    for j in range(fbuf.shape[0]):
        fbuf[j] = rows[:, j * 128:(j + 1) * 128].astype(F32)
    for l in range(2):
        for j in range(fbuf.shape[0]):
            qbuf[l, :, j * 128:(j + 1) * 128] = fbuf[
                j, pl.ds(l, qpd, stride=2), :
            ].astype(BF16)

    for off in range(1, n):
        arrived(off).wait_recv()

    t = tbuf[...].astype(F32)
    energy = jnp.sum(t * t, axis=0) * (1.0 / n)
    first = lax.broadcasted_iota(jnp.int32, energy.shape, 1) < rank
    sum0 = jnp.sum(jnp.where(first, energy, 0.0))
    sum1 = jnp.sum(jnp.where(first, 0.0, energy))
    damping = jnp.where(first, sum0, sum1) * (0.1 / (rank * rank)) + 1e-6
    scaled = t * (1.0 / (energy + damping))[None]
    y = dot3(scaled.reshape(n * rank, 2 * rank), right, NT)
    wide = 2 * rank
    lanes = lax.broadcasted_iota(jnp.int32, (n, wide), 1) < rank
    total = None
    for l in range(2):
        yl = jnp.concatenate(
            [y[s * rank:(s + 1) * rank, l * wide:(l + 1) * wide] for s in range(n)], axis=1
        )
        w = dot3(frames_out[l], yl)
        for s in range(n):
            wbuf[l, s * rank:(s + 1) * rank, :] = w[:, s * wide:(s + 1) * wide]
        tiles = []
        for j in range(rank // 2):
            even = wbuf[l, pl.ds(2 * j, n, stride=rank), :]
            odd = wbuf[l, pl.ds(2 * j + 1, n, stride=rank), :]
            tiles.append(jnp.where(lanes, even, odd))
        flat = jnp.concatenate(tiles, axis=1)
        hi = flat.astype(BF16).astype(F32)
        both = jnp.concatenate([hi, flat - hi], axis=0).astype(BF16)
        p = dot(both, qbuf[l], NT)
        p = p[:n] + p[n:]
        total = p if total is None else total + p
    if qpd < 128:
        total = jnp.concatenate([total, jnp.zeros((n, 128 - qpd), F32)], axis=1)
    for s in range(n):
        sbuf[s] = total[s:s + 1]

    slot = core * half + lax.rem(me, half)

    def deliver(off):
        to = lax.rem(me + off, n)
        return pltpu.make_async_remote_copy(
            src_ref=sbuf.at[to], dst_ref=rbuf.at[slot],
            send_sem=send2_sem.at[off], recv_sem=recv2_sem.at[slot],
            device_id=(part, to, mine), device_id_type=MESH,
        )

    for off in range(1, n):
        deliver(off).start()

    @pl.when(mine == core)
    def _():
        rbuf[slot] = sbuf[me]

    @pl.when(mine != core)
    def _():
        deliver(0).start()

    for lay in range(layers):
        for j in range(half):
            src = core * half + j
            own = jnp.logical_and(src == me, core == lay)

            @pl.when(jnp.logical_not(own))
            def _(lay=lay, j=j):
                k = lay * half + j
                pltpu.make_async_remote_copy(
                    src_ref=sbuf.at[0], dst_ref=rbuf.at[k],
                    send_sem=send2_sem.at[0], recv_sem=recv2_sem.at[k],
                    device_id=(part, me, mine), device_id_type=MESH,
                ).wait_recv()

    pieces = []
    for j in range(half):
        acc = rbuf[j]
        for lay in range(1, layers):
            acc = acc + rbuf[lay * half + j]
        pieces.append(acc[:, :qpd])
    out[...] = jnp.concatenate(pieces, axis=1)

    for off in range(1, n):
        gather(off).wait_send()
        deliver(off).wait_send()

    @pl.when(mine != core)
    def _():
        deliver(0).wait_send()


def per_device(acts, grads, lens, query, pin, pout, bin_, bout, lids):
    n = lax.axis_size("dp")
    layers = lax.axis_size("layer")
    _, held, tokens, width = acts.shape
    rank = pin.shape[1]
    qpd = query.shape[0]
    hbm = pl.BlockSpec(memory_space=pl.ANY)
    smem = pl.BlockSpec(memory_space=pltpu.SMEM)
    return pl.pallas_call(
        functools.partial(kernel, n, layers),
        out_shape=jax.ShapeDtypeStruct((1, n * qpd // layers), F32),
        in_specs=[smem, smem] + [hbm] * 7,
        out_specs=pl.BlockSpec(memory_space=pltpu.VMEM),
        scratch_shapes=[
            pltpu.VMEM((held, tokens, width), BF16),
            pltpu.VMEM((held, tokens, width), BF16),
            pltpu.VMEM(pin.shape, BF16),
            pltpu.VMEM(pin.shape, BF16),
            pltpu.VMEM(query.shape, BF16),
            pltpu.VMEM((query.shape[2] // 128, qpd * held, 128), F32),
            pltpu.VMEM((held, qpd, query.shape[2]), BF16),
            pltpu.VMEM(bin_.shape, F32),
            pltpu.VMEM(bout.shape, F32),
            pltpu.VMEM((n, rank, held * rank), BF16),
            pltpu.VMEM((held, n * rank, 2 * rank), F32),
            pltpu.VMEM((n, 1, 128), F32),
            pltpu.VMEM((n, 1, 128), F32),
            pltpu.SemaphoreType.DMA((11,)),
            pltpu.SemaphoreType.DMA((n - 1,)),
            pltpu.SemaphoreType.DMA((n - 1,)),
            pltpu.SemaphoreType.DMA((n,)),
            pltpu.SemaphoreType.DMA((n,)),
        ],
        compiler_params=pltpu.CompilerParams(
            collective_id=0, has_side_effects=True, vmem_limit_bytes=60 * 2**20
        ),
    )(lens, lids, acts, grads, query, pin, pout, bin_, bout)


def solution(mesh):
    return jax.shard_map(
        per_device,
        mesh=mesh,
        in_specs=(
            P(("parts", "dp"), "layer", None, None),
            P(("parts", "dp"), "layer", None, None),
            P(("parts", "dp")),
            P("dp", "layer", None),
            P("layer", None, None),
            P("layer", None, None),
            P(),
            P(),
            P("layer"),
        ),
        out_specs=P(("parts", "dp"), "layer"),
        check_vma=False,
    )
```

```python
import functools

import jax
import jax.numpy as jnp
from jax import lax
from jax.experimental import pallas as pl
from jax.experimental.pallas import tpu as pltpu
from jax.sharding import PartitionSpec as P

F32 = jnp.float32
BF16 = jnp.bfloat16
CHUNK = 256
WINDOW = 4
MESH = pl.DeviceIdType.MESH
NN = (((1,), (0,)), ((), ()))
NT = (((1,), (1,)), ((), ()))


def dot(a, b, dims=NN):
    return lax.dot_general(a, b, dims, preferred_element_type=F32)


def split(a):
    hi = a.astype(BF16)
    return hi, (a - hi.astype(F32)).astype(BF16)


def dot3(a, b, dims=NN):
    ah, al = split(a)
    bh, bl = split(b)
    return dot(ah, bh, dims) + (dot(ah, bl, dims) + dot(al, bh, dims))


def deep3(a, b):
    ah, al = split(a)
    bh, bl = split(b)
    return dot(jnp.concatenate([ah, ah, al], axis=1), jnp.concatenate([bh, bl, bh], axis=0))


def kernel(
    n, layers, lens, lids, acts, grads, query, pin, pout, bin_, bout, out,
    abuf, gbuf, pibuf, pobuf, xbuf, fbuf, qbuf, bibuf, bobuf, tbuf, wbuf, sbuf, rbuf,
    load_sem, send_sem, recv_sem, send2_sem, recv2_sem,
):
    part = lax.axis_index("parts")
    me = lax.axis_index("dp")
    core = lax.axis_index("layer")
    half = n // layers
    mine = me // half
    rank = pibuf.shape[1]
    qpd = query.shape[0]
    tokens = abuf.shape[1]

    barrier = pltpu.get_barrier_semaphore()
    for off in range(n):
        for lay in range(layers):
            if off == 0 and lay == 0:
                continue
            pl.semaphore_signal(
                barrier, inc=1,
                device_id=(part, lax.rem(me + off, n), lax.rem(core + lay, layers)),
                device_id_type=MESH,
            )

    plan = []
    for l in range(2):
        for weights, held, rows, kept in ((pout, pobuf, grads, gbuf), (pin, pibuf, acts, abuf)):
            plan.append((weights.at[l], held.at[l]))
            for c in range(0, tokens, CHUNK):
                plan.append((rows.at[0, l, c:c + CHUNK], kept.at[l, c:c + CHUNK]))
    plan += [(bin_, bibuf), (bout, bobuf), (query, xbuf)]
    loads = [
        pltpu.make_async_copy(src, dst, load_sem.at[i]) for i, (src, dst) in enumerate(plan)
    ]
    for copy in loads[:WINDOW]:
        copy.start()
    count = [0]

    def landed():
        i = count[0]
        loads[i].wait()
        if i + WINDOW < len(loads):
            loads[i + WINDOW].start()
        count[0] = i + 1

    length = lens[0]
    live = lax.broadcasted_iota(jnp.int32, (rank, tokens), 1) < length
    lows = []
    for l in range(2):
        landed()
        low_out = []
        for c in range(0, tokens, CHUNK):
            landed()
            low_out.append(dot(pobuf[l], gbuf[l, c:c + CHUNK], NT))
        landed()
        low_in = []
        for c in range(0, tokens, CHUNK):
            landed()
            low_in.append(dot(abuf[l, c:c + CHUNK], pibuf[l], NT))
        low_out = jnp.where(live, jnp.concatenate(low_out, axis=1), 0.0)
        lows.append((low_out, jnp.concatenate(low_in, axis=0)))
    outers = [dot3(low_out, low_in) for low_out, low_in in lows]
    landed()
    landed()
    frames_in = [bibuf[lids[l]] for l in range(2)]
    frames_out = [bobuf[lids[l]] for l in range(2)]
    lefts = [deep3(frames_out[l].T, outers[l]) for l in range(2)]
    turned = [dot3(lefts[l], frames_in[l]) for l in range(2)]
    tbuf[me] = jnp.concatenate(turned, axis=1).astype(BF16)

    peers = (n * layers) - 1
    pl.semaphore_wait(barrier, peers)

    def gather(off):
        to = lax.rem(me + off, n)
        return pltpu.make_async_remote_copy(
            src_ref=tbuf.at[me], dst_ref=tbuf.at[me],
            send_sem=send_sem.at[off - 1], recv_sem=recv_sem.at[off - 1],
            device_id=(part, to, core), device_id_type=MESH,
        )

    def arrived(off):
        frm = lax.rem(me + n - off, n)
        return pltpu.make_async_remote_copy(
            src_ref=tbuf.at[frm], dst_ref=tbuf.at[frm],
            send_sem=send_sem.at[off - 1], recv_sem=recv_sem.at[off - 1],
            device_id=(part, frm, core), device_id_type=MESH,
        )

    for off in range(1, n):
        gather(off).start()

    zero = jnp.zeros((rank, rank), F32)
    v0 = jnp.concatenate([frames_in[0], zero], axis=1)
    v1 = jnp.concatenate([zero, frames_in[1]], axis=1)
    right = jnp.concatenate([v0, v0, v1, v1], axis=0)
    landed()
    rows = xbuf[...].reshape(2 * qpd, xbuf.shape[2])
    for j in range(fbuf.shape[0]):
        fbuf[j] = rows[:, j * 128:(j + 1) * 128].astype(F32)
    for l in range(2):
        for j in range(fbuf.shape[0]):
            qbuf[l, :, j * 128:(j + 1) * 128] = fbuf[
                j, pl.ds(l, qpd, stride=2), :
            ].astype(BF16)

    for off in range(1, n):
        arrived(off).wait_recv()

    t = tbuf[...].astype(F32)
    energy = jnp.sum(t * t, axis=0) * (1.0 / n)
    first = lax.broadcasted_iota(jnp.int32, energy.shape, 1) < rank
    sum0 = jnp.sum(jnp.where(first, energy, 0.0))
    sum1 = jnp.sum(jnp.where(first, 0.0, energy))
    damping = jnp.where(first, sum0, sum1) * (0.1 / (rank * rank)) + 1e-6
    scaled = t * (1.0 / (energy + damping))[None]
    y = dot3(scaled.reshape(n * rank, 2 * rank), right, NT)
    wide = 2 * rank
    lanes = lax.broadcasted_iota(jnp.int32, (n, wide), 1) < rank
    total = None
    for l in range(2):
        yl = jnp.concatenate(
            [y[s * rank:(s + 1) * rank, l * wide:(l + 1) * wide] for s in range(n)], axis=1
        )
        w = deep3(frames_out[l], yl)
        for s in range(n):
            wbuf[l, s * rank:(s + 1) * rank, :] = w[:, s * wide:(s + 1) * wide]
        tiles = []
        for j in range(rank // 2):
            even = wbuf[l, pl.ds(2 * j, n, stride=rank), :]
            odd = wbuf[l, pl.ds(2 * j + 1, n, stride=rank), :]
            tiles.append(jnp.where(lanes, even, odd))
        flat = jnp.concatenate(tiles, axis=1)
        hi = flat.astype(BF16).astype(F32)
        both = jnp.concatenate([hi, flat - hi], axis=0).astype(BF16)
        p = dot(both, qbuf[l], NT)
        p = p[:n] + p[n:]
        total = p if total is None else total + p
    if qpd < 128:
        total = jnp.concatenate([total, jnp.zeros((n, 128 - qpd), F32)], axis=1)
    for s in range(n):
        sbuf[s] = total[s:s + 1]

    slot = core * half + lax.rem(me, half)

    def deliver(off):
        to = lax.rem(me + off, n)
        return pltpu.make_async_remote_copy(
            src_ref=sbuf.at[to], dst_ref=rbuf.at[slot],
            send_sem=send2_sem.at[off], recv_sem=recv2_sem.at[slot],
            device_id=(part, to, mine), device_id_type=MESH,
        )

    for off in range(1, n):
        deliver(off).start()

    @pl.when(mine == core)
    def _():
        rbuf[slot] = sbuf[me]

    @pl.when(mine != core)
    def _():
        deliver(0).start()

    for lay in range(layers):
        for j in range(half):
            src = core * half + j
            own = jnp.logical_and(src == me, core == lay)

            @pl.when(jnp.logical_not(own))
            def _(lay=lay, j=j):
                k = lay * half + j
                pltpu.make_async_remote_copy(
                    src_ref=sbuf.at[0], dst_ref=rbuf.at[k],
                    send_sem=send2_sem.at[0], recv_sem=recv2_sem.at[k],
                    device_id=(part, me, mine), device_id_type=MESH,
                ).wait_recv()

    pieces = []
    for j in range(half):
        acc = rbuf[j]
        for lay in range(1, layers):
            acc = acc + rbuf[lay * half + j]
        pieces.append(acc[:, :qpd])
    out[...] = jnp.concatenate(pieces, axis=1)

    for off in range(1, n):
        gather(off).wait_send()
        deliver(off).wait_send()

    @pl.when(mine != core)
    def _():
        deliver(0).wait_send()


def per_device(acts, grads, lens, query, pin, pout, bin_, bout, lids):
    n = lax.axis_size("dp")
    layers = lax.axis_size("layer")
    _, held, tokens, width = acts.shape
    rank = pin.shape[1]
    qpd = query.shape[0]
    hbm = pl.BlockSpec(memory_space=pl.ANY)
    smem = pl.BlockSpec(memory_space=pltpu.SMEM)
    return pl.pallas_call(
        functools.partial(kernel, n, layers),
        out_shape=jax.ShapeDtypeStruct((1, n * qpd // layers), F32),
        in_specs=[smem, smem] + [hbm] * 7,
        out_specs=pl.BlockSpec(memory_space=pltpu.VMEM),
        scratch_shapes=[
            pltpu.VMEM((held, tokens, width), BF16),
            pltpu.VMEM((held, tokens, width), BF16),
            pltpu.VMEM(pin.shape, BF16),
            pltpu.VMEM(pin.shape, BF16),
            pltpu.VMEM(query.shape, BF16),
            pltpu.VMEM((query.shape[2] // 128, qpd * held, 128), F32),
            pltpu.VMEM((held, qpd, query.shape[2]), BF16),
            pltpu.VMEM(bin_.shape, F32),
            pltpu.VMEM(bout.shape, F32),
            pltpu.VMEM((n, rank, held * rank), BF16),
            pltpu.VMEM((held, n * rank, 2 * rank), F32),
            pltpu.VMEM((n, 1, 128), F32),
            pltpu.VMEM((n, 1, 128), F32),
            pltpu.SemaphoreType.DMA((4 + 4 * (tokens // CHUNK) + 3,)),
            pltpu.SemaphoreType.DMA((n - 1,)),
            pltpu.SemaphoreType.DMA((n - 1,)),
            pltpu.SemaphoreType.DMA((n,)),
            pltpu.SemaphoreType.DMA((n,)),
        ],
        compiler_params=pltpu.CompilerParams(
            collective_id=0, has_side_effects=True, vmem_limit_bytes=60 * 2**20
        ),
    )(lens, lids, acts, grads, query, pin, pout, bin_, bout)


def solution(mesh):
    return jax.shard_map(
        per_device,
        mesh=mesh,
        in_specs=(
            P(("parts", "dp"), "layer", None, None),
            P(("parts", "dp"), "layer", None, None),
            P(("parts", "dp")),
            P("dp", "layer", None),
            P("layer", None, None),
            P("layer", None, None),
            P(),
            P(),
            P("layer"),
        ),
        out_specs=P(("parts", "dp"), "layer"),
        check_vma=False,
    )
```

```python
import functools

import jax
import jax.numpy as jnp
from jax import lax
from jax.experimental import pallas as pl
from jax.experimental.pallas import tpu as pltpu
from jax.sharding import PartitionSpec as P

F32 = jnp.float32
BF16 = jnp.bfloat16
CHUNK = 256
WINDOW = 4
MESH = pl.DeviceIdType.MESH
NN = (((1,), (0,)), ((), ()))
NT = (((1,), (1,)), ((), ()))


def dot(a, b, dims=NN):
    return lax.dot_general(a, b, dims, preferred_element_type=F32)


def split(a):
    hi = a.astype(BF16)
    return hi, (a - hi.astype(F32)).astype(BF16)


def dot3(a, b, dims=NN):
    ah, al = split(a)
    bh, bl = split(b)
    return dot(ah, bh, dims) + (dot(ah, bl, dims) + dot(al, bh, dims))


def deep3(a, b):
    ah, al = split(a)
    bh, bl = split(b)
    return dot(jnp.concatenate([ah, ah, al], axis=1), jnp.concatenate([bh, bl, bh], axis=0))


def kernel(
    n, layers, lens_hbm, lids_hbm, acts, grads, query, pin, pout, bin_, bout, out,
    abuf, gbuf, pibuf, pobuf, xbuf, fbuf, qbuf, bibuf, bobuf, tbuf, wbuf, sbuf, rbuf,
    lens, lids, id_sem, load_sem, send_sem, recv_sem, send2_sem, recv2_sem,
):
    part = lax.axis_index("parts")
    me = lax.axis_index("dp")
    core = lax.axis_index("layer")
    half = n // layers
    mine = me // half
    rank = pibuf.shape[1]
    qpd = query.shape[0]
    tokens = abuf.shape[1]

    plan = []
    for l in range(2):
        for weights, held, rows, kept in ((pout, pobuf, grads, gbuf), (pin, pibuf, acts, abuf)):
            plan.append((weights.at[l], held.at[l]))
            for c in range(0, tokens, CHUNK):
                plan.append((rows.at[0, l, c:c + CHUNK], kept.at[l, c:c + CHUNK]))
    plan += [(bin_, bibuf), (bout, bobuf), (query, xbuf)]
    loads = [
        pltpu.make_async_copy(src, dst, load_sem.at[i]) for i, (src, dst) in enumerate(plan)
    ]
    ids = [
        pltpu.make_async_copy(lens_hbm, lens, id_sem.at[0]),
        pltpu.make_async_copy(lids_hbm, lids, id_sem.at[1]),
    ]
    for copy in ids + loads[:WINDOW]:
        copy.start()
    barrier = pltpu.get_barrier_semaphore()
    for off in range(n):
        for lay in range(layers):
            if off == 0 and lay == 0:
                continue
            pl.semaphore_signal(
                barrier, inc=1,
                device_id=(part, lax.rem(me + off, n), lax.rem(core + lay, layers)),
                device_id_type=MESH,
            )

    count = [0]

    def landed():
        i = count[0]
        loads[i].wait()
        if i + WINDOW < len(loads):
            loads[i + WINDOW].start()
        count[0] = i + 1

    for copy in ids:
        copy.wait()
    length = lens[0]
    live = lax.broadcasted_iota(jnp.int32, (rank, tokens), 1) < length
    lows = []
    for l in range(2):
        landed()
        low_out = []
        for c in range(0, tokens, CHUNK):
            landed()
            low_out.append(dot(pobuf[l], gbuf[l, c:c + CHUNK], NT))
        landed()
        low_in = []
        for c in range(0, tokens, CHUNK):
            landed()
            low_in.append(dot(abuf[l, c:c + CHUNK], pibuf[l], NT))
        low_out = jnp.where(live, jnp.concatenate(low_out, axis=1), 0.0)
        lows.append((low_out, jnp.concatenate(low_in, axis=0)))
    outers = [dot3(low_out, low_in) for low_out, low_in in lows]
    landed()
    landed()
    frames_in = [bibuf[lids[l]] for l in range(2)]
    frames_out = [bobuf[lids[l]] for l in range(2)]
    lefts = [deep3(frames_out[l].T, outers[l]) for l in range(2)]
    turned = [dot3(lefts[l], frames_in[l]) for l in range(2)]
    tbuf[me] = jnp.concatenate(turned, axis=1).astype(BF16)

    peers = (n * layers) - 1
    pl.semaphore_wait(barrier, peers)

    def gather(off):
        to = lax.rem(me + off, n)
        return pltpu.make_async_remote_copy(
            src_ref=tbuf.at[me], dst_ref=tbuf.at[me],
            send_sem=send_sem.at[off - 1], recv_sem=recv_sem.at[off - 1],
            device_id=(part, to, core), device_id_type=MESH,
        )

    def arrived(off):
        frm = lax.rem(me + n - off, n)
        return pltpu.make_async_remote_copy(
            src_ref=tbuf.at[frm], dst_ref=tbuf.at[frm],
            send_sem=send_sem.at[off - 1], recv_sem=recv_sem.at[off - 1],
            device_id=(part, frm, core), device_id_type=MESH,
        )

    for off in range(1, n):
        gather(off).start()

    zero = jnp.zeros((rank, rank), F32)
    v0 = jnp.concatenate([frames_in[0], zero], axis=1)
    v1 = jnp.concatenate([zero, frames_in[1]], axis=1)
    right = jnp.concatenate([v0, v0, v1, v1], axis=0)
    landed()
    rows = xbuf[...].reshape(2 * qpd, xbuf.shape[2])
    for j in range(fbuf.shape[0]):
        fbuf[j] = rows[:, j * 128:(j + 1) * 128].astype(F32)
    for l in range(2):
        for j in range(fbuf.shape[0]):
            qbuf[l, :, j * 128:(j + 1) * 128] = fbuf[
                j, pl.ds(l, qpd, stride=2), :
            ].astype(BF16)

    for off in range(1, n):
        arrived(off).wait_recv()

    t = tbuf[...].astype(F32)
    energy = jnp.sum(t * t, axis=0) * (1.0 / n)
    first = lax.broadcasted_iota(jnp.int32, energy.shape, 1) < rank
    sum0 = jnp.sum(jnp.where(first, energy, 0.0))
    sum1 = jnp.sum(jnp.where(first, 0.0, energy))
    damping = jnp.where(first, sum0, sum1) * (0.1 / (rank * rank)) + 1e-6
    scaled = t * (1.0 / (energy + damping))[None]
    y = dot3(scaled.reshape(n * rank, 2 * rank), right, NT)
    wide = 2 * rank
    lanes = lax.broadcasted_iota(jnp.int32, (n, wide), 1) < rank
    total = None
    for l in range(2):
        yl = jnp.concatenate(
            [y[s * rank:(s + 1) * rank, l * wide:(l + 1) * wide] for s in range(n)], axis=1
        )
        w = deep3(frames_out[l], yl)
        for s in range(n):
            wbuf[l, s * rank:(s + 1) * rank, :] = w[:, s * wide:(s + 1) * wide]
        tiles = []
        for j in range(rank // 2):
            even = wbuf[l, pl.ds(2 * j, n, stride=rank), :]
            odd = wbuf[l, pl.ds(2 * j + 1, n, stride=rank), :]
            tiles.append(jnp.where(lanes, even, odd))
        flat = jnp.concatenate(tiles, axis=1)
        hi = flat.astype(BF16).astype(F32)
        both = jnp.concatenate([hi, flat - hi], axis=0).astype(BF16)
        p = dot(both, qbuf[l], NT)
        p = p[:n] + p[n:]
        total = p if total is None else total + p
    if qpd < 128:
        total = jnp.concatenate([total, jnp.zeros((n, 128 - qpd), F32)], axis=1)
    for s in range(n):
        sbuf[s] = total[s:s + 1]

    slot = core * half + lax.rem(me, half)

    def deliver(off):
        to = lax.rem(me + off, n)
        return pltpu.make_async_remote_copy(
            src_ref=sbuf.at[to], dst_ref=rbuf.at[slot],
            send_sem=send2_sem.at[off], recv_sem=recv2_sem.at[slot],
            device_id=(part, to, mine), device_id_type=MESH,
        )

    for off in range(1, n):
        deliver(off).start()

    @pl.when(mine == core)
    def _():
        rbuf[slot] = sbuf[me]

    @pl.when(mine != core)
    def _():
        deliver(0).start()

    for lay in range(layers):
        for j in range(half):
            src = core * half + j
            own = jnp.logical_and(src == me, core == lay)

            @pl.when(jnp.logical_not(own))
            def _(lay=lay, j=j):
                k = lay * half + j
                pltpu.make_async_remote_copy(
                    src_ref=sbuf.at[0], dst_ref=rbuf.at[k],
                    send_sem=send2_sem.at[0], recv_sem=recv2_sem.at[k],
                    device_id=(part, me, mine), device_id_type=MESH,
                ).wait_recv()

    pieces = []
    for j in range(half):
        acc = rbuf[j]
        for lay in range(1, layers):
            acc = acc + rbuf[lay * half + j]
        pieces.append(acc[:, :qpd])
    out[...] = jnp.concatenate(pieces, axis=1)

    for off in range(1, n):
        gather(off).wait_send()
        deliver(off).wait_send()

    @pl.when(mine != core)
    def _():
        deliver(0).wait_send()


def per_device(acts, grads, lens, query, pin, pout, bin_, bout, lids):
    n = lax.axis_size("dp")
    layers = lax.axis_size("layer")
    _, held, tokens, width = acts.shape
    rank = pin.shape[1]
    qpd = query.shape[0]
    hbm = pl.BlockSpec(memory_space=pl.ANY)
    return pl.pallas_call(
        functools.partial(kernel, n, layers),
        out_shape=jax.ShapeDtypeStruct((1, n * qpd // layers), F32),
        in_specs=[hbm] * 9,
        out_specs=pl.BlockSpec(memory_space=pltpu.VMEM),
        scratch_shapes=[
            pltpu.VMEM((held, tokens, width), BF16),
            pltpu.VMEM((held, tokens, width), BF16),
            pltpu.VMEM(pin.shape, BF16),
            pltpu.VMEM(pin.shape, BF16),
            pltpu.VMEM(query.shape, BF16),
            pltpu.VMEM((query.shape[2] // 128, qpd * held, 128), F32),
            pltpu.VMEM((held, qpd, query.shape[2]), BF16),
            pltpu.VMEM(bin_.shape, F32),
            pltpu.VMEM(bout.shape, F32),
            pltpu.VMEM((n, rank, held * rank), BF16),
            pltpu.VMEM((held, n * rank, 2 * rank), F32),
            pltpu.VMEM((n, 1, 128), F32),
            pltpu.VMEM((n, 1, 128), F32),
            pltpu.SMEM(lens.shape, jnp.int32),
            pltpu.SMEM(lids.shape, jnp.int32),
            pltpu.SemaphoreType.DMA((2,)),
            pltpu.SemaphoreType.DMA((4 + 4 * (tokens // CHUNK) + 3,)),
            pltpu.SemaphoreType.DMA((n - 1,)),
            pltpu.SemaphoreType.DMA((n - 1,)),
            pltpu.SemaphoreType.DMA((n,)),
            pltpu.SemaphoreType.DMA((n,)),
        ],
        compiler_params=pltpu.CompilerParams(
            collective_id=0, has_side_effects=True, vmem_limit_bytes=60 * 2**20
        ),
    )(lens, lids, acts, grads, query, pin, pout, bin_, bout)


def solution(mesh):
    return jax.shard_map(
        per_device,
        mesh=mesh,
        in_specs=(
            P(("parts", "dp"), "layer", None, None),
            P(("parts", "dp"), "layer", None, None),
            P(("parts", "dp")),
            P("dp", "layer", None),
            P("layer", None, None),
            P("layer", None, None),
            P(),
            P(),
            P("layer"),
        ),
        out_specs=P(("parts", "dp"), "layer"),
        check_vma=False,
    )
```

```python
import functools

import jax
import jax.numpy as jnp
from jax import lax
from jax.experimental import pallas as pl
from jax.experimental.pallas import tpu as pltpu
from jax.sharding import PartitionSpec as P

F32 = jnp.float32
BF16 = jnp.bfloat16
CHUNK = 256
WINDOW = 4
MESH = pl.DeviceIdType.MESH
NN = (((1,), (0,)), ((), ()))
NT = (((1,), (1,)), ((), ()))


def dot(a, b, dims=NN):
    return lax.dot_general(a, b, dims, preferred_element_type=F32)


def split(a):
    hi = a.astype(BF16)
    return hi, (a - hi.astype(F32)).astype(BF16)


def dot3(a, b, dims=NN):
    ah, al = split(a)
    bh, bl = split(b)
    return dot(ah, bh, dims) + (dot(ah, bl, dims) + dot(al, bh, dims))


def deep3(a, b):
    ah, al = split(a)
    bh, bl = split(b)
    return dot(jnp.concatenate([ah, ah, al], axis=1), jnp.concatenate([bh, bl, bh], axis=0))


def kernel(
    n, layers, lens_hbm, lids_hbm, acts, grads, query, pin, pout, bin_, bout, out,
    abuf, gbuf, pibuf, pobuf, xbuf, fbuf, qbuf, bibuf, bobuf, tbuf, wbuf, sbuf, rbuf,
    lens, lids, id_sem, load_sem, send_sem, recv_sem, send2_sem, recv2_sem,
):
    part = lax.axis_index("parts")
    me = lax.axis_index("dp")
    core = lax.axis_index("layer")
    half = n // layers
    mine = me // half
    rank = pibuf.shape[1]
    qpd = query.shape[0]
    tokens = abuf.shape[1]

    plan = []
    for l in range(2):
        for weights, held, rows, kept in ((pout, pobuf, grads, gbuf), (pin, pibuf, acts, abuf)):
            plan.append((weights.at[l], held.at[l]))
            for c in range(0, tokens, CHUNK):
                plan.append((rows.at[0, l, c:c + CHUNK], kept.at[l, c:c + CHUNK]))
    plan += [(bin_, bibuf), (bout, bobuf), (query, xbuf)]
    loads = [
        pltpu.make_async_copy(src, dst, load_sem.at[i]) for i, (src, dst) in enumerate(plan)
    ]
    ids = [
        pltpu.make_async_copy(lens_hbm, lens, id_sem.at[0]),
        pltpu.make_async_copy(lids_hbm, lids, id_sem.at[1]),
    ]
    for copy in ids + loads[:WINDOW]:
        copy.start()
    barrier = pltpu.get_barrier_semaphore()
    for off in range(n):
        for lay in range(layers):
            if off == 0 and lay == 0:
                continue
            pl.semaphore_signal(
                barrier, inc=1,
                device_id=(part, lax.rem(me + off, n), lax.rem(core + lay, layers)),
                device_id_type=MESH,
            )

    count = [0]

    def landed():
        i = count[0]
        loads[i].wait()
        if i + WINDOW < len(loads):
            loads[i + WINDOW].start()
        count[0] = i + 1

    for copy in ids:
        copy.wait()
    length = lens[0]
    live = lax.broadcasted_iota(jnp.int32, (rank, tokens), 1) < length
    lows = []
    for l in range(2):
        landed()
        low_out = []
        for c in range(0, tokens, CHUNK):
            landed()
            low_out.append(dot(pobuf[l], gbuf[l, c:c + CHUNK], NT))
        landed()
        low_in = []
        for c in range(0, tokens, CHUNK):
            landed()
            low_in.append(dot(abuf[l, c:c + CHUNK], pibuf[l], NT))
        low_out = jnp.where(live, jnp.concatenate(low_out, axis=1), 0.0)
        lows.append((low_out, jnp.concatenate(low_in, axis=0)))
    outers = [dot3(low_out, low_in) for low_out, low_in in lows]
    landed()
    landed()
    frames_in = [bibuf[lids[l]] for l in range(2)]
    frames_out = [bobuf[lids[l]] for l in range(2)]
    lefts = [deep3(frames_out[l].T, outers[l]) for l in range(2)]
    turned = [dot3(lefts[l], frames_in[l]) for l in range(2)]
    tbuf[me] = jnp.concatenate(turned, axis=1).astype(BF16)

    peers = (n * layers) - 1
    pl.semaphore_wait(barrier, peers)

    def gather(off):
        to = lax.rem(me + off, n)
        return pltpu.make_async_remote_copy(
            src_ref=tbuf.at[me], dst_ref=tbuf.at[me],
            send_sem=send_sem.at[off - 1], recv_sem=recv_sem.at[off - 1],
            device_id=(part, to, core), device_id_type=MESH,
        )

    def arrived(off):
        frm = lax.rem(me + n - off, n)
        return pltpu.make_async_remote_copy(
            src_ref=tbuf.at[frm], dst_ref=tbuf.at[frm],
            send_sem=send_sem.at[off - 1], recv_sem=recv_sem.at[off - 1],
            device_id=(part, frm, core), device_id_type=MESH,
        )

    for off in range(1, n):
        gather(off).start()

    zero = jnp.zeros((rank, rank), F32)
    v0 = jnp.concatenate([frames_in[0], zero], axis=1)
    v1 = jnp.concatenate([zero, frames_in[1]], axis=1)
    right_hi, right_lo = split(jnp.concatenate([v0, v0, v1, v1], axis=0))
    right_twice = jnp.concatenate([right_hi, right_hi], axis=1)
    landed()
    rows = xbuf[...].reshape(2 * qpd, xbuf.shape[2])
    for j in range(fbuf.shape[0]):
        fbuf[j] = rows[:, j * 128:(j + 1) * 128].astype(F32)
    for l in range(2):
        for j in range(fbuf.shape[0]):
            qbuf[l, :, j * 128:(j + 1) * 128] = fbuf[
                j, pl.ds(l, qpd, stride=2), :
            ].astype(BF16)

    for off in range(1, n):
        arrived(off).wait_recv()

    t = tbuf[...].astype(F32)
    energy = jnp.sum(t * t, axis=0) * (1.0 / n)
    first = lax.broadcasted_iota(jnp.int32, energy.shape, 1) < rank
    sum0 = jnp.sum(jnp.where(first, energy, 0.0))
    sum1 = jnp.sum(jnp.where(first, 0.0, energy))
    damping = jnp.where(first, sum0, sum1) * (0.1 / (rank * rank)) + 1e-6
    scaled = t * (1.0 / (energy + damping))[None]
    sh, sl = split(scaled.reshape(n * rank, 2 * rank))
    y = dot(jnp.concatenate([sh, sl], axis=1), right_twice, NT) + dot(sh, right_lo, NT)
    wide = 2 * rank
    lanes = lax.broadcasted_iota(jnp.int32, (n, wide), 1) < rank
    total = None
    for l in range(2):
        yl = jnp.concatenate(
            [y[s * rank:(s + 1) * rank, l * wide:(l + 1) * wide] for s in range(n)], axis=1
        )
        w = deep3(frames_out[l], yl)
        for s in range(n):
            wbuf[l, s * rank:(s + 1) * rank, :] = w[:, s * wide:(s + 1) * wide]
        tiles = []
        for j in range(rank // 2):
            even = wbuf[l, pl.ds(2 * j, n, stride=rank), :]
            odd = wbuf[l, pl.ds(2 * j + 1, n, stride=rank), :]
            tiles.append(jnp.where(lanes, even, odd))
        flat = jnp.concatenate(tiles, axis=1)
        hi = flat.astype(BF16).astype(F32)
        both = jnp.concatenate([hi, flat - hi], axis=0).astype(BF16)
        p = dot(both, qbuf[l], NT)
        p = p[:n] + p[n:]
        total = p if total is None else total + p
    if qpd < 128:
        total = jnp.concatenate([total, jnp.zeros((n, 128 - qpd), F32)], axis=1)
    for s in range(n):
        sbuf[s] = total[s:s + 1]

    slot = core * half + lax.rem(me, half)

    def deliver(off):
        to = lax.rem(me + off, n)
        return pltpu.make_async_remote_copy(
            src_ref=sbuf.at[to], dst_ref=rbuf.at[slot],
            send_sem=send2_sem.at[off], recv_sem=recv2_sem.at[slot],
            device_id=(part, to, mine), device_id_type=MESH,
        )

    for off in range(1, n):
        deliver(off).start()

    @pl.when(mine == core)
    def _():
        rbuf[slot] = sbuf[me]

    @pl.when(mine != core)
    def _():
        deliver(0).start()

    for lay in range(layers):
        for j in range(half):
            src = core * half + j
            own = jnp.logical_and(src == me, core == lay)

            @pl.when(jnp.logical_not(own))
            def _(lay=lay, j=j):
                k = lay * half + j
                pltpu.make_async_remote_copy(
                    src_ref=sbuf.at[0], dst_ref=rbuf.at[k],
                    send_sem=send2_sem.at[0], recv_sem=recv2_sem.at[k],
                    device_id=(part, me, mine), device_id_type=MESH,
                ).wait_recv()

    pieces = []
    for j in range(half):
        acc = rbuf[j]
        for lay in range(1, layers):
            acc = acc + rbuf[lay * half + j]
        pieces.append(acc[:, :qpd])
    out[...] = jnp.concatenate(pieces, axis=1)

    for off in range(1, n):
        gather(off).wait_send()
        deliver(off).wait_send()

    @pl.when(mine != core)
    def _():
        deliver(0).wait_send()


def per_device(acts, grads, lens, query, pin, pout, bin_, bout, lids):
    n = lax.axis_size("dp")
    layers = lax.axis_size("layer")
    _, held, tokens, width = acts.shape
    rank = pin.shape[1]
    qpd = query.shape[0]
    hbm = pl.BlockSpec(memory_space=pl.ANY)
    return pl.pallas_call(
        functools.partial(kernel, n, layers),
        out_shape=jax.ShapeDtypeStruct((1, n * qpd // layers), F32),
        in_specs=[hbm] * 9,
        out_specs=pl.BlockSpec(memory_space=pltpu.VMEM),
        scratch_shapes=[
            pltpu.VMEM((held, tokens, width), BF16),
            pltpu.VMEM((held, tokens, width), BF16),
            pltpu.VMEM(pin.shape, BF16),
            pltpu.VMEM(pin.shape, BF16),
            pltpu.VMEM(query.shape, BF16),
            pltpu.VMEM((query.shape[2] // 128, qpd * held, 128), F32),
            pltpu.VMEM((held, qpd, query.shape[2]), BF16),
            pltpu.VMEM(bin_.shape, F32),
            pltpu.VMEM(bout.shape, F32),
            pltpu.VMEM((n, rank, held * rank), BF16),
            pltpu.VMEM((held, n * rank, 2 * rank), F32),
            pltpu.VMEM((n, 1, 128), F32),
            pltpu.VMEM((n, 1, 128), F32),
            pltpu.SMEM(lens.shape, jnp.int32),
            pltpu.SMEM(lids.shape, jnp.int32),
            pltpu.SemaphoreType.DMA((2,)),
            pltpu.SemaphoreType.DMA((4 + 4 * (tokens // CHUNK) + 3,)),
            pltpu.SemaphoreType.DMA((n - 1,)),
            pltpu.SemaphoreType.DMA((n - 1,)),
            pltpu.SemaphoreType.DMA((n,)),
            pltpu.SemaphoreType.DMA((n,)),
        ],
        compiler_params=pltpu.CompilerParams(
            collective_id=0, has_side_effects=True, vmem_limit_bytes=60 * 2**20
        ),
    )(lens, lids, acts, grads, query, pin, pout, bin_, bout)


def solution(mesh):
    return jax.shard_map(
        per_device,
        mesh=mesh,
        in_specs=(
            P(("parts", "dp"), "layer", None, None),
            P(("parts", "dp"), "layer", None, None),
            P(("parts", "dp")),
            P("dp", "layer", None),
            P("layer", None, None),
            P("layer", None, None),
            P(),
            P(),
            P("layer"),
        ),
        out_specs=P(("parts", "dp"), "layer"),
        check_vma=False,
    )
```
